512 devices in a mesh: dp: 32 (over z, y_lo), expert: 16 (over x, y_hi, core).
Axes of the slice: x: 4, y: 4 (y_hi: 2, y_lo: 2; y = y_hi * 2 + y_lo), z: 16, core: 2. Of those that a mesh axis runs over, the one named last changes fastest.
Arguments:
- out_grad: bfloat16 [2048, 6144], P('expert', 'dp'), may hold values from -6 to 6
- hidden: bfloat16 [16, 1024, 5376], P('expert', None, 'dp'), may hold values from -0.59765625 to 0.59765625
- down_weight: bfloat16 [16, 5376, 6144], P('expert', 'dp'), may hold values from -0.078125 to 0.078125
- experts: int32 [2048, 4], replicated, may hold values from 0 to 15, all different within a row; in each aligned block of 128 rows (0 to 127, 128 to 255, ...) at most 64 rows name the same one
- route_weight: float32 [2048, 4], replicated, may hold values from 0.05 to 1
Outputs:
- hidden_grad: bfloat16 [16, 1024, 5376], P('expert', None, 'dp')
- weight_grad: bfloat16 [16, 5376, 6144], P('expert', 'dp')
- route_grad: float32 [2048, 4], P('expert')
The draws below stay inside these ranges and needn't reach their ends.
Inputs may be any that keep to these rules, and one draw needn't show every extreme that they name: The 4 experts of a token differ; among the tokens of one aligned block of 128 tokens no expert is named by more than 64 of them.
All inputs are finite; a program needn't handle non-finite values.
Results may differ from the reference program's by a relative error of at most 0.0049.
Values may be sent and summed in bfloat16 or wider, within the bound.
A program may use at most 64 MiB of HBM per device.

```python
import math
import jax
import jax.numpy as jnp
import numpy as np
from jax import lax

D = 6144
FF = 5376
TOK_DEV = 128
EXPERTS = 16
TOPK = 4
TOKENS = 2048
MOST = 64
CAP = 1024


def steps_of(stream_key, dims, shards, smallest, high):
    factor_of = 1.0
    for axis_at, shards_of in shards:
        draws = jax.random.uniform(jax.random.fold_in(jax.random.fold_in(stream_key, 6), axis_at), (shards_of,), jnp.float32, smallest / len(shards), high / len(shards))
        factor_of = factor_of * jnp.repeat(jnp.exp(draws), dims[axis_at] // shards_of).reshape((-1,) + (1,) * (len(dims) - 1 - axis_at))
    return factor_of


def deal_out(key, own, number, rows, number_of, top, reach, skew):
    sequence = jax.random.permutation(key, number_of)
    heavy_load, usual = portions_of(number_of, rows * top, reach, skew, True), portions_of(number_of, rows * top, reach, skew, False)
    places = jnp.arange(number_of)

    def named(sizes, rotation):
        used = int((sizes > 0).sum())
        fixed = max(1, used // 4)
        passed = fixed + (places - fixed + rotation * (used - fixed)) % max(1, number_of - fixed)
        return jnp.zeros((number_of,), jnp.int32).at[sequence[jnp.where(places < fixed, places, passed)]].set(jnp.asarray(sizes, jnp.int32))

    sizes = jnp.where(number % 4 == 0, named(heavy_load, number // 4), named(usual, number - number // 4 - 1))
    mixed = jax.random.permutation(jax.random.fold_in(own, 3), number_of)
    donor, taker = mixed[0:number_of // 2 * 2:2], mixed[1:number_of // 2 * 2:2]
    slack = jnp.minimum(sizes[donor] - 1, reach - sizes[taker]) // 2
    slack = jnp.where((donor == sequence[0]) | (taker == sequence[0]) | (sizes[taker] == 0), 0, jnp.maximum(slack, 0))
    passed = jax.random.randint(jax.random.fold_in(own, 4), (number_of // 2,), 0, 1 << 20) % (slack + 1)
    sizes = sizes.at[donor].add(-passed).at[taker].add(passed)
    labels = jnp.searchsorted(jnp.cumsum(sizes), jnp.arange(rows * top), side="right").astype(jnp.int32)
    listing = labels.reshape(top, rows).T
    listing = listing[jax.random.permutation(jax.random.fold_in(own, 1), rows)]
    rotation = jax.random.randint(jax.random.fold_in(own, 2), (rows, 1), 0, top)
    return jnp.take_along_axis(listing, (jnp.arange(top)[None, :] + rotation) % top, axis=1)


def portions_of(amount, total, bound, lean, full):
    portions = [(1 << 20) // math.isqrt(standing ** lean) + 1 for standing in range(1, amount + 1)]
    largest = bound if full else min(bound, max(-(-total // amount), total * portions[0] // sum(portions)))
    least = 1 if total - largest >= amount - 1 else 0
    given, surplus = [largest] + [least] * (amount - 1), total - largest - least * (amount - 1)
    while surplus > 0:
        movable = [i for i in range(1, amount) if given[i] < largest] or [i for i in range(1, amount) if given[i] < bound]
        pool, budget = sum([portions[i] for i in movable]), surplus
        for i in movable:
            extra = min(bound - given[i], max(1, budget * portions[i] // pool), surplus)
            given[i] = given[i] + extra
            surplus = surplus - extra
    return np.array(given)


def bell_draw(rng, shape, width, limit, shards=(), kind=jnp.bfloat16):
    factor_of = steps_of(rng, shape, shards, -0.22, 0.18) if shards else 1.0
    array = jax.random.normal(rng, shape, jnp.float32) * width * factor_of
    return jnp.minimum(jnp.maximum(array, -limit), limit).astype(kind)


def setup_inputs(seed: int = 0) -> dict:
    streams_of = jax.random.split(jax.random.key(seed), 6)
    out_grad = bell_draw(streams_of[0], (TOKENS, D), 1.0, 6.0, ((0, 16), (1, 32)))
    hidden = bell_draw(streams_of[1], (EXPERTS, CAP, FF), 0.1, 0.59765625, ((0, 16), (2, 32)))
    down_weight = bell_draw(streams_of[2], (EXPERTS, FF, D), FF ** -0.5, 0.078125, ((0, 16), (1, 32)))
    experts_keys = jax.random.split(jax.random.fold_in(streams_of[3], 1), TOKENS // TOK_DEV)
    experts_turns = jax.random.permutation(jax.random.fold_in(streams_of[3], 3), TOKENS // TOK_DEV)
    experts = jax.vmap(lambda own, number: deal_out(jax.random.fold_in(streams_of[3], 2), own, number, TOK_DEV, EXPERTS, TOPK, MOST, 2))(experts_keys, experts_turns).reshape((TOKENS, TOPK))
    route_weight = jnp.clip(jnp.exp(jax.random.uniform(streams_of[4], (TOKENS, TOPK), jnp.float32, math.log(0.05), math.log(1.0))), 0.05, 1.0)
    return dict(out_grad=out_grad, hidden=hidden, down_weight=down_weight, experts=experts, route_weight=route_weight)


def reference(out_grad, hidden, down_weight, experts, route_weight):
    blocks = TOKENS // TOK_DEV
    match = experts[:, :, None] == jnp.arange(EXPERTS).astype(jnp.int32)[None, None, :]
    tok_hit = jnp.any(match, axis=1).astype(jnp.int32)
    tok_weight = jnp.sum(jnp.where(match, route_weight[:, :, None], jnp.zeros_like(route_weight)[:, :, None]), axis=1)
    block_hit = tok_hit.reshape(blocks, TOK_DEV, EXPERTS)
    rank = (jnp.cumsum(block_hit, axis=1) - 1).astype(jnp.int32)
    marks = (block_hit[..., None] == 1) & (rank[..., None] == jnp.arange(MOST).astype(jnp.int32))
    positions = jnp.arange(TOK_DEV).astype(jnp.int32)[None, :, None, None]
    local = jnp.sum(jnp.where(marks, positions, 0), axis=1).astype(jnp.int32)
    live = jnp.any(marks, axis=1)
    slot_weight = jnp.sum(jnp.where(marks, tok_weight.reshape(blocks, TOK_DEV, EXPERTS, 1), jnp.zeros_like(tok_weight)[0, 0]), axis=1)
    starts = (jnp.arange(blocks).astype(jnp.int32) * TOK_DEV)[:, None, None]
    slot_token = jnp.transpose(starts + local, (1, 0, 2)).reshape(EXPERTS, CAP).astype(jnp.int32)
    live = jnp.transpose(live, (1, 0, 2)).reshape(EXPERTS, CAP)
    slot_weight = jnp.transpose(slot_weight, (1, 0, 2)).reshape(EXPERTS, CAP)

    def one_expert(items):
        token_ids, live_e, weight_e, saved, matrix = items
        rows = jnp.where(live_e[:, None], out_grad[token_ids], jnp.zeros((), out_grad.dtype)).astype(jnp.bfloat16)
        raw = lax.dot_general(rows, matrix, (((1,), (1,)), ((), ())), preferred_element_type=jnp.float32)
        grad_hidden = (weight_e[:, None] * raw).astype(jnp.bfloat16)
        scaled = (weight_e[:, None] * rows.astype(jnp.float32)).astype(jnp.bfloat16)
        grad_weight = lax.dot_general(saved, scaled, (((0,), (0,)), ((), ())), preferred_element_type=jnp.float32).astype(jnp.bfloat16)
        slot_grad = jnp.sum(saved.astype(jnp.float32) * raw, axis=1)
        return grad_hidden, grad_weight, slot_grad

    hidden_grad, weight_grad, slot_grad = lax.map(one_expert, (slot_token, live, slot_weight, hidden, down_weight))
    rank_flat = rank.reshape(TOKENS, EXPERTS)
    route_rank = jnp.take_along_axis(rank_flat, experts, axis=1).astype(jnp.int32)
    slots = ((jnp.arange(TOKENS).astype(jnp.int32) // TOK_DEV)[:, None] * MOST + route_rank).astype(jnp.int32)
    route_grad = slot_grad[experts, slots]
    return hidden_grad, weight_grad, route_grad
```

```python
import functools

import jax
import jax.numpy as jnp
from jax import lax
from jax.experimental import pallas as pl
from jax.experimental.pallas import tpu as pltpu
from jax.sharding import PartitionSpec as P

MESH = pl.DeviceIdType.MESH
F32, BF16 = jnp.float32, jnp.bfloat16

X, Y, Z = 4, 4, 16
HALF = 64
FEAT = 384
BLOCKS = 16
TOK = 128
FFD = 168
MOST = 64
GROUPS = 9


def kernel(
    og_ref, hid_ref, w_ref, ex_ref, rw_ref,
    hg_ref, wg_ref, rt_ref,
    rows, raw, hwt, sel, code, wtok, half, sg, sgx, red,
    px_s, px_r, u_s, u_r, z_s, z_r, v_s, v_r, a_s, a_r, c_s, c_r, x_s, x_r, d_s, d_r,
):
    dp, ex = lax.axis_index("dp"), lax.axis_index("expert")
    z, ylo = dp // 2, dp % 2
    x, yhi, c = ex // 4, (ex // 2) % 2, ex % 2
    y = yhi * 2 + ylo
    u = y + c * (x - y)
    v = x + c * (y - x)

    def at(x, y, z, c):
        return {"dp": z * 2 + y % 2, "expert": (x * 2 + y // 2) * 2 + c}

    def along(du, dv):
        uu, vv = (u + du + 4) % 4, (v + dv + 4) % 4
        return at(vv + c * (uu - vv), uu + c * (vv - uu), z, c)

    def beside(dz):
        return at(x, y, (z + dz + Z) % Z, c)

    twin = at(x, y, z, 1 - c)
    pair = {"dp": dp + 1 - 2 * ylo, "expert": ex}

    barrier = pltpu.get_barrier_semaphore()
    greeted = [along(k, 0) for k in (1, 2, 3)] + [along(0, k) for k in (1, 2, 3)]
    greeted += [beside(1), beside(-1), twin]
    for device in greeted:
        pl.semaphore_signal(barrier, inc=1, device_id=device, device_id_type=MESH)
    pl.semaphore_wait(barrier, len(greeted))

    sent = []

    def copy(src, dst, send, recv, device):
        return pltpu.make_async_remote_copy(
            src_ref=src, dst_ref=dst, send_sem=send, recv_sem=recv, device_id=device, device_id_type=MESH
        )

    def push(src, dst, send, recv, device):
        op = copy(src, dst, send, recv, device)
        op.start()
        sent.append(op)

    def arrived(dst, send, recv):
        copy(dst, dst, send, recv, twin).wait_recv()

    push(og_ref.at[pl.ds((1 - ylo) * HALF, HALF)], half, px_s, px_r, pair)
    arrived(half, px_s, px_r)
    mine = og_ref[pl.ds(ylo * HALF, HALF), :].astype(F32)
    theirs = half[...].astype(F32)
    first = jnp.where(ylo == 0, mine, theirs)
    second = jnp.where(ylo == 0, theirs, mine)
    rows[0, c, v, u] = jnp.concatenate([first, second], axis=1).astype(BF16)

    for k in (1, 2, 3):
        own = rows.at[0, c, v, u]
        push(own, own, u_s.at[k - 1], u_r.at[k - 1], along(k, 0))
    for k in (1, 2, 3):
        arrived(rows.at[0, c, v, (u - k + 4) % 4], u_s.at[k - 1], u_r.at[k - 1])

    def z_part(slot, part):
        return rows.at[slot, c, v, pl.ds(2 * part, 2)]

    def z_send(d):
        for part in (0, 1):
            for way in (0, 1):
                if d == 7 and way != part:
                    continue
                src = 0 if d == 0 else 2 * d - 1 + way
                dst = 15 if d == 7 else 2 * d + 1 + way
                push(z_part(src, part), z_part(dst, part), z_s.at[d, way, part], z_r.at[d, way, part], beside(1 - 2 * way))

    def z_wait(d):
        for part in (0, 1):
            for way in (0, 1):
                if d == 8 and way != part:
                    continue
                dst = 15 if d == 8 else 2 * d - 1 + way
                arrived(z_part(dst, part), z_s.at[d - 1, way, part], z_r.at[d - 1, way, part])

    def slots(d):
        return pl.ds(0, 1) if d == 0 else pl.ds(15, 1) if d == 8 else pl.ds(2 * d - 1, 2)

    def v_all(d, vv):
        return rows.at[slots(d), c, vv]

    def v_half(d, vv, way):
        if d in (0, 8):
            return rows.at[slots(d), c, vv, pl.ds(2 * way, 2)]
        return rows.at[pl.ds(2 * d - 1 + way, 1), c, vv]

    def v_send(d):
        for way in (0, 1):
            own = v_all(d, v)
            push(own, own, v_s.at[d, way], v_r.at[d, way], along(0, 1 - 2 * way))

    def v_pass(d):
        for way in (0, 1):
            step = 1 - 2 * way
            vv = (v - step + 4) % 4
            arrived(v_all(d, vv), v_s.at[d, way], v_r.at[d, way])
            part = v_half(d, vv, way)
            push(part, part, a_s.at[d, way], a_r.at[d, way], along(0, step))

    def c_send(d):
        vv = (v + 2) % 4
        for way in (0, 1):
            arrived(v_half(d, vv, way), a_s.at[d, way], a_r.at[d, way])
        own = rows.at[slots(d), c]
        push(own, own, c_s.at[d], c_r.at[d], twin)

    def c_wait(d):
        arrived(rows.at[slots(d), 1 - c], c_s.at[d], c_r.at[d])

    def prepare():
        hit = jnp.zeros((BLOCKS, TOK), jnp.bool_)
        weight = jnp.zeros((BLOCKS, TOK), F32)
        for k in range(4):
            mine = ex_ref[k] == ex
            hit = hit | mine
            weight = weight + jnp.where(mine, rw_ref[k], 0.0)
        upto = lax.broadcasted_iota(jnp.int32, (TOK, TOK), 0) <= lax.broadcasted_iota(jnp.int32, (TOK, TOK), 1)
        count = jnp.dot(
            jnp.where(hit, 1.0, 0.0).astype(BF16), jnp.where(upto, 1.0, 0.0).astype(BF16), preferred_element_type=F32
        )
        code[...] = jnp.where(hit, count - 1.0, -1.0)
        wtok[...] = weight
        slot = lax.broadcasted_iota(jnp.int32, (MOST, TOK), 0).astype(F32)
        lane = lax.broadcasted_iota(jnp.int32, (FFD, TOK), 1)

        def block(b):
            one = jnp.where(slot == code[pl.ds(b, 1), :], 1.0, 0.0)
            sel[b] = one.astype(BF16)
            w = jnp.sum(one * wtok[pl.ds(b, 1), :], axis=1, keepdims=True)
            hid = hid_ref[0, pl.ds(b * MOST, MOST), :]
            hidw = (hid.astype(F32) * w).astype(BF16)
            return lax.dot_general(hidw, one.astype(BF16), (((0,), (0,)), ((), ())), preferred_element_type=F32)

        def plane0(i, _):
            hwt[i] = block(i * 2).astype(BF16)
            return 0

        lax.fori_loop(0, 8, plane0, 0)

        def plane1(i, _):
            xh, yh = i // 2, i % 2
            b0 = xh * 8 + yh * 2 + 1
            left, right = block(b0), block(b0 + 4)
            low = jnp.where(lane < HALF, left, pltpu.roll(right, HALF, 1))
            high = jnp.where(lane < HALF, pltpu.roll(left, HALF, 1), right)
            hwt[8 + yh * 4 + xh] = low.astype(BF16)
            hwt[8 + yh * 4 + 2 + xh] = high.astype(BF16)
            return 0

        lax.fori_loop(0, 4, plane1, 0)
        raw[...] = jnp.zeros_like(raw)

    def places(d):
        if d == 0:
            return ((0, z),)
        if d == 8:
            return ((15, (z + 8) % Z),)
        return ((2 * d - 1, (z - d + Z) % Z), (2 * d, (z + d) % Z))

    def columns(zi):
        return pl.ds(pl.multiple_of(zi * FEAT, 128), FEAT)

    def add_raw(d):
        here = places(d)
        w = jnp.concatenate([w_ref[0, :, columns(zi)] for _, zi in here], axis=1)

        def tile(i, _):
            t = jnp.concatenate([rows[s, i // 4, i % 4].reshape(4 * HALF, FEAT) for s, _ in here], axis=1)
            raw[i] += lax.dot_general(t, w, (((1,), (1,)), ((), ())), preferred_element_type=F32)
            return 0

        lax.fori_loop(0, 8, tile, 0)

    def put_grad(d):
        for s, zi in places(d):
            left = jnp.concatenate([hwt[i] for i in range(16)], axis=1)
            t = rows[s].reshape(2 * X * Y * HALF, FEAT)
            wg_ref[0, :, columns(zi)] = jnp.dot(left, t, preferred_element_type=F32).astype(BF16)

    z_send(0)
    v_send(0)
    prepare()
    for d in range(1, GROUPS + 3):
        if d <= 8:
            z_wait(d)
            if d < 8:
                z_send(d)
            v_send(d)
        if 0 <= d - 1 <= 8:
            v_pass(d - 1)
        if 0 <= d - 2 <= 8:
            c_send(d - 2)
        if 0 <= d - 3 <= 8:
            c_wait(d - 3)
            add_raw(d - 3)
            if d - 3 < 8:
                put_grad(d - 3)

    def block_out(b, row0, row1):
        part = jnp.concatenate([row0, row1], axis=0)
        high = part.astype(BF16)
        low = (part - high.astype(F32)).astype(BF16)
        one = sel[b]
        mine = jnp.dot(one, high, preferred_element_type=F32) + jnp.dot(one, low, preferred_element_type=F32)
        onef = one.astype(F32)
        w = jnp.sum(onef * wtok[pl.ds(b, 1), :], axis=1, keepdims=True)
        at_b = pl.ds(b * MOST, MOST)
        hg_ref[0, at_b, :] = (w * mine).astype(BF16)
        slot_grad = jnp.sum(hid_ref[0, at_b, :].astype(F32) * mine, axis=1, keepdims=True)
        sg[b] = jnp.broadcast_to(jnp.sum(slot_grad * onef, axis=0, keepdims=True), (8, TOK))

    def out0(i, _):
        at_i = pl.multiple_of((i % 2) * TOK, TOK)
        block_out(i * 2, raw[i // 2, pl.ds(at_i, HALF), :], raw[i // 2, pl.ds(at_i + HALF, HALF), :])
        return 0

    def out1(i, _):
        xx, yh = i // 2, i % 2
        at_i = pl.multiple_of(xx * HALF, HALF)
        block_out(i * 2 + 1, raw[4 + 2 * yh, pl.ds(at_i, HALF), :], raw[5 + 2 * yh, pl.ds(at_i, HALF), :])
        return 0

    lax.fori_loop(0, 8, out0, 0)
    lax.fori_loop(0, 8, out1, 0)

    for k in range(1, BLOCKS):
        to = (ex + k) % BLOCKS
        push(sg.at[to], sgx.at[ex], x_s.at[k], x_r.at[k], {"dp": dp, "expert": to})
    put_grad(8)
    sgx[ex] = sg[ex]
    for k in range(1, BLOCKS):
        arrived(sgx.at[(ex - k + BLOCKS) % BLOCKS], x_s.at[k], x_r.at[k])
    share = []
    for k in range(4):
        named = ex_ref[k, pl.ds(ex, 1), :]
        total = jnp.zeros((1, TOK), F32)
        for e in range(BLOCKS):
            total = total + jnp.where(named == e, sgx[e, 0:1, :], 0.0)
        share.append(total)
    red[dp] = jnp.concatenate(share, axis=0)
    for k in range(1, 2 * Z):
        own = red.at[dp]
        push(own, own, d_s.at[k], d_r.at[k], {"dp": (dp + k) % (2 * Z), "expert": ex})
    for k in range(1, 2 * Z):
        arrived(red.at[(dp - k + 2 * Z) % (2 * Z)], d_s.at[k], d_r.at[k])
    total = red[0]
    for k in range(1, 2 * Z):
        total = total + red[k]
    rt_ref[...] = total
    for op in sent:
        op.wait_send()


def body(out_grad, hidden, down_weight, experts, route_weight):
    experts_t = experts.T.reshape(4, BLOCKS, TOK)
    weight_t = route_weight.T.reshape(4, BLOCKS, TOK)
    vmem = pl.BlockSpec(memory_space=pltpu.VMEM)
    dma = pltpu.SemaphoreType.DMA
    hidden_grad, weight_grad, route = pl.pallas_call(
        kernel,
        out_shape=(
            jax.ShapeDtypeStruct(hidden.shape, BF16),
            jax.ShapeDtypeStruct(down_weight.shape, BF16),
            jax.ShapeDtypeStruct((4, TOK), F32),
        ),
        in_specs=[vmem] * 5,
        out_specs=(vmem,) * 3,
        scratch_shapes=[
            pltpu.VMEM((Z, 2, 4, 4, HALF, FEAT), BF16),
            pltpu.VMEM((8, 4 * HALF, FFD), F32),
            pltpu.VMEM((16, FFD, TOK), BF16),
            pltpu.VMEM((BLOCKS, MOST, TOK), BF16),
            pltpu.VMEM((BLOCKS, TOK), F32),
            pltpu.VMEM((BLOCKS, TOK), F32),
            pltpu.VMEM((HALF, 192), BF16),
            pltpu.VMEM((BLOCKS, 8, TOK), F32),
            pltpu.VMEM((BLOCKS, 8, TOK), F32),
            pltpu.VMEM((2 * Z, 4, TOK), F32),
            dma, dma,
            dma((3,)), dma((3,)),
            dma((8, 2, 2)), dma((8, 2, 2)),
            dma((GROUPS, 2)), dma((GROUPS, 2)),
            dma((GROUPS, 2)), dma((GROUPS, 2)),
            dma((GROUPS,)), dma((GROUPS,)),
            dma((BLOCKS,)), dma((BLOCKS,)),
            dma((2 * Z,)), dma((2 * Z,)),
        ],
        compiler_params=pltpu.CompilerParams(
            collective_id=0, has_side_effects=True, vmem_limit_bytes=56 << 20
        ),
        cost_estimate=pl.CostEstimate(flops=8 * 10**9, bytes_accessed=30 * 10**6, transcendentals=0),
        name="broadcast_grads",
    )(out_grad, hidden, down_weight, experts_t, weight_t)
    return hidden_grad, weight_grad, route.T


def solution(mesh):
    placed = (P("expert", "dp"), P("expert", None, "dp"), P("expert", "dp", None), P(), P())
    return jax.shard_map(
        body,
        mesh=mesh,
        in_specs=placed,
        out_specs=(P("expert", None, "dp"), P("expert", "dp", None), P("expert", None)),
        check_vma=False,
    )
```

```python
import jax
import jax.numpy as jnp
from jax import lax
from jax.experimental import pallas as pl
from jax.experimental.pallas import tpu as pltpu
from jax.sharding import PartitionSpec as P

MESH = pl.DeviceIdType.MESH
F32, BF16 = jnp.float32, jnp.bfloat16

Z = 16
PIECE = 192
FEAT = 384
BLOCKS = 16
TOK = 128
TOKENS = BLOCKS * TOK
FFD = 168
MOST = 64
GROUPS = 9
NT = (((1,), (1,)), ((), ()))
ORDER = (0, 1, 3, 2)
EARLY = (0, 1, 2)
EARLY_SLOTS = (0, 1, 2, 3, 4)
SKIP = 4
LATE = (4, 7, 8)

PLAN = (
    "U1", "U3", "Z10", "U2", "Z11", "Z13", "P0", "Z12", "Z20", "Z21", "Z23", "L0", "Z22", "P1", "Z30", "Z31", "R0",
    "Z33", "G0", "Z32", "P2", "Z40", "L1", "Z41", "Z43", "Z42", "R1", "Z50", "Z51", "P3", "Z53", "G1", "Z52", "L2",
    "E0", "Z60", "Z61", "L3", "R2", "Z63", "Z62", "R3", "P5", "Z70", "E1", "F0", "G2", "Z71", "E2", "G3", "Z73", "Z72",
    "Z80", "P6", "E3", "F1", "L5", "Z81", "E4", "Z83", "F2", "Z82", "R5", "P7", "E5", "F3", "G5", "L6", "F4", "P8",
    "R6", "F5", "L7", "G6", "L8", "R4", "R7", "R8",
)


def kernel(
    og_ref, hid_hbm, w_hbm, ex_hbm, rw_hbm,
    hg_ref, wg_ref, rt_ref,
    hid_ref, w_ref, ex_ref, rw_ref,
    rows, raw, ht, hw, sel, wtok, sg, sgx, red,
    load, u_s, u_r, z_s, z_r, p_s, p_r, e_s, e_r, v_s, v_r, a_s, a_r, c_s, c_r, x_s, x_r, d_s, d_r,
):
    dp, ex = lax.axis_index("dp"), lax.axis_index("expert")
    z, ylo = dp // 2, dp % 2
    x, yhi, c = ex // 4, (ex // 2) % 2, ex % 2
    y = yhi * 2 + ylo
    u = y + c * (x - y)
    v = x + c * (y - x)

    def at(x, y, z, c):
        return {"dp": z * 2 + y % 2, "expert": (x * 2 + y // 2) * 2 + c}

    def along(du, dv):
        uu, vv = (u + du + 4) % 4, (v + dv + 4) % 4
        return at(vv + c * (uu - vv), uu + c * (vv - uu), z, c)

    def beside(dz):
        return at(x, y, (z + dz + Z) % Z, c)

    twin = at(x, y, z, 1 - c)

    loads = [
        pltpu.make_async_copy(src, dst, load.at[i])
        for i, (src, dst) in enumerate(
            ((ex_hbm, ex_ref), (rw_hbm, rw_ref), (hid_hbm, hid_ref), (w_hbm, w_ref))
        )
    ]
    for op in loads:
        op.start()

    barrier = pltpu.get_barrier_semaphore()
    greeted = [along(k, 0) for k in (1, 2, 3)] + [along(0, k) for k in (1, 3)]
    greeted += [beside(1), beside(-1), twin]
    for device in greeted:
        pl.semaphore_signal(barrier, inc=1, device_id=device, device_id_type=MESH)
    pl.semaphore_wait(barrier, len(greeted))

    sent = []

    def copy(src, dst, send, recv, device):
        return pltpu.make_async_remote_copy(
            src_ref=src, dst_ref=dst, send_sem=send, recv_sem=recv, device_id=device, device_id_type=MESH
        )

    def push(src, dst, send, recv, device):
        op = copy(src, dst, send, recv, device)
        op.start()
        sent.append(op)

    def arrived(dst, send, recv):
        copy(dst, dst, send, recv, twin).wait_recv()


    def piece(slot, vv, k):
        return rows.at[slot, c, vv, (u - k + 4) % 4]

    def z_send(d, k):
        for way in (0, 1):
            if d == 7 and way != k // 2:
                continue
            src = 0 if d == 0 else 2 * d - 1 + way
            dst = 15 if d == 7 else 2 * d + 1 + way
            own = og_ref if d == 0 and k == 0 else piece(src, v, k)
            push(own, piece(dst, v, k), z_s.at[d, way, k], z_r.at[d, way, k], beside(1 - 2 * way))

    def z_wait(d, k):
        for way in (0, 1):
            if d == 8 and way != k // 2:
                continue
            dst = 15 if d == 8 else 2 * d - 1 + way
            arrived(piece(dst, v, k), z_s.at[d - 1, way, k], z_r.at[d - 1, way, k])

    def slot_list(d):
        return (0,) if d == 0 else (15,) if d == 8 else (2 * d - 1, 2 * d)

    def slots(d):
        return pl.ds(0, 1) if d == 0 else pl.ds(15, 1) if d == 8 else pl.ds(2 * d - 1, 2)

    def v_all(d, vv):
        return rows.at[slots(d), c, vv]

    def v_half(d, vv, way):
        if d in (0, 8):
            return rows.at[slots(d), c, vv, pl.ds(2 * way, 2)]
        return rows.at[pl.ds(2 * d - 1 + way, 1), c, vv]

    def v_send(d):
        for way in (0, 1):
            own = v_all(d, v)
            push(own, own, v_s.at[d, way], v_r.at[d, way], along(0, 1 - 2 * way))

    def v_piece(slot, k):
        at_slot = EARLY_SLOTS.index(slot)
        for way in (0, 1):
            own = og_ref if slot == 0 and k == 0 else piece(slot, v, k)
            push(own, piece(slot, v, k), p_s.at[at_slot, k, way], p_r.at[at_slot, k, way], along(0, 1 - 2 * way))

    def v_pass(d):
        for way in (0, 1):
            step = 1 - 2 * way
            vv = (v - step + 4) % 4
            if d in EARLY:
                for slot in slot_list(d):
                    for k in ORDER:
                        at_slot = EARLY_SLOTS.index(slot)
                        arrived(piece(slot, vv, k), p_s.at[at_slot, k, way], p_r.at[at_slot, k, way])
            else:
                arrived(v_all(d, vv), v_s.at[d, way], v_r.at[d, way])
            half = v_half(d, vv, way)
            push(half, half, a_s.at[d, way], a_r.at[d, way], along(0, step))

    def v_last(d):
        for way in (0, 1):
            arrived(v_half(d, (v + 2) % 4, way), a_s.at[d, way], a_r.at[d, way])

    def e_part(slot, unit):
        return rows.at[slot, c, (v + (1, 3, 2)[unit // 2]) % 4, pl.ds(2 * (unit % 2), 2)]

    def e_send(unit):
        for way in (0, 1):
            src, dst = e_part(2 * SKIP - 3 + way, unit), e_part(2 * SKIP - 1 + way, unit)
            push(src, dst, e_s.at[way, unit], e_r.at[way, unit], beside(1 - 2 * way))

    def e_wait(unit):
        for way in (0, 1):
            arrived(e_part(2 * SKIP - 1 + way, unit), e_s.at[way, unit], e_r.at[way, unit])

    def c_send(d, k):
        own = rows.at[slots(d), c, (v + k) % 4]
        push(own, own, c_s.at[d, k], c_r.at[d, k], twin)

    def c_wait(d):
        for k in range(4):
            arrived(rows.at[slots(d), 1 - c, (u + k) % 4], c_s.at[d, k], c_r.at[d, k])

    def prepare():
        mine = ex_ref[...] == ex
        hit = jnp.max(jnp.where(mine, 1.0, 0.0), axis=0, keepdims=True)
        wtok[...] = jnp.sum(jnp.where(mine, rw_ref[...], 0.0), axis=0, keepdims=True)
        hits = jnp.concatenate([hit[:, b * TOK : (b + 1) * TOK] for b in range(BLOCKS)], axis=0)
        upto = lax.broadcasted_iota(jnp.int32, (TOK, TOK), 0) <= lax.broadcasted_iota(jnp.int32, (TOK, TOK), 1)
        count = jnp.dot(hits.astype(BF16), jnp.where(upto, 1.0, 0.0).astype(BF16), preferred_element_type=F32)
        code = jnp.where(hits > 0, count - 1.0, -1000.0)
        slot = lax.broadcasted_iota(jnp.int32, (2 * MOST, 2 * TOK), 0).astype(F32)
        for j in range(BLOCKS // 2):
            both = jnp.concatenate([code[2 * j : 2 * j + 1], code[2 * j + 1 : 2 * j + 2] + float(MOST)], axis=1)
            one = jnp.where(slot == both, 1.0, 0.0).astype(BF16)
            sel[j] = one
            tokens = pl.ds(j * 2 * TOK, 2 * TOK)
            part = jnp.dot(hid_ref[0, :, pl.ds(j * TOK, TOK)], one, preferred_element_type=F32)
            ht[:, tokens] = part.astype(BF16)
            hw[:, tokens] = (part * wtok[:, tokens]).astype(BF16)

    def places(d):
        if d == 0:
            return ((0, z),)
        if d == 8:
            return ((15, (z + 8) % Z),)
        return ((2 * d - 1, (z - d + Z) % Z), (2 * d, (z + d) % Z))

    def columns(zi):
        return pl.ds(pl.multiple_of(zi * FEAT, 128), FEAT)

    def slab(s, xx):
        cols = []
        for b in range(4):
            yh = b // 2
            if b % 2 == 0:
                cols.append(rows[s, 0, xx, 2 * yh : 2 * yh + 2].reshape(FEAT, TOK))
            else:
                cols.append(jnp.concatenate([rows[s, 1, 2 * yh, xx], rows[s, 1, 2 * yh + 1, xx]], axis=0))
        return jnp.concatenate(cols, axis=1)

    def add_raw(d, first):
        here = places(d)
        w = jnp.concatenate([w_ref[0, :, columns(zi)] for _, zi in here], axis=1)

        def tile(xx, _):
            t = jnp.concatenate([slab(s, xx) for s, _ in here], axis=0)
            tokens = pl.ds(pl.multiple_of(xx * 4 * TOK, 4 * TOK), 4 * TOK)
            more = jnp.dot(w, t, preferred_element_type=F32)
            raw[:, tokens] = more if first else raw[:, tokens] + more
            return 0

        lax.fori_loop(0, 4, tile, 0)

    def put_grad(d):
        for s, zi in places(d):
            t = jnp.concatenate([slab(s, xx) for xx in range(4)], axis=1)
            wg_ref[0, :, columns(zi)] = lax.dot_general(hw[...], t, NT, preferred_element_type=F32).astype(BF16)

    for k in (1, 3, 2):
        push(og_ref, piece(0, v, 0), u_s.at[k - 1], u_r.at[k - 1], along(k, 0))
    z_send(0, 0)
    v_piece(0, 0)
    rows[0, c, v, u] = og_ref[...]
    for op in loads[:3]:
        op.wait()
    prepare()
    loads[3].wait()

    def on_u(k):
        arrived(piece(0, v, k), u_s.at[k - 1], u_r.at[k - 1])
        z_send(0, k)
        v_piece(0, k)
        if k == ORDER[3]:
            c_send(0, 0)

    def on_z(d, k):
        z_wait(d, k)
        if d < 8:
            z_send(d, k)
        if d in EARLY:
            for slot in slot_list(d):
                v_piece(slot, k)
        if k == ORDER[3]:
            if d not in EARLY and d != SKIP:
                v_send(d)
            c_send(d, 0)

    def on_v(d):
        v_pass(d)
        c_send(d, 1)
        c_send(d, 3)

    def on_far(d):
        v_last(d)
        c_send(d, 2)

    def on_e(unit):
        e_wait(unit)
        if unit % 2 == 1:
            c_send(SKIP, (1, 3, 2)[unit // 2])

    summed = []
    for step in PLAN:
        kind, d = step[0], int(step[1])
        if kind == "U":
            on_u(d)
        elif kind == "Z":
            on_z(d, int(step[2]))
        elif kind == "P":
            on_v(d)
        elif kind == "L":
            on_far(d)
        elif kind == "E":
            e_send(d)
        elif kind == "F":
            on_e(d)
        elif kind == "R":
            c_wait(d)
            add_raw(d, not summed)
            summed.append(d)
        else:
            put_grad(d)

    share = jnp.sum(ht[...].astype(F32) * raw[...], axis=0, keepdims=True)
    for b in range(BLOCKS):
        sg[b] = jnp.broadcast_to(share[:, b * TOK : (b + 1) * TOK], (8, TOK))
    for k in range(1, BLOCKS):
        to = (ex + k) % BLOCKS
        push(sg.at[to], sgx.at[ex], x_s.at[k], x_r.at[k], {"dp": dp, "expert": to})
    sgx[ex] = sg[ex]
    for d in LATE[::2]:
        put_grad(d)
    named = ex_ref[:, pl.ds(pl.multiple_of(ex * TOK, TOK), TOK)]
    total = jnp.zeros((4, TOK), F32)
    for k in range(1, BLOCKS):
        arrived(sgx.at[(ex - k + BLOCKS) % BLOCKS], x_s.at[k], x_r.at[k])
    for e in range(BLOCKS):
        total = total + jnp.where(named == e, sgx[e, 0:1, :], 0.0)
    red[dp] = total
    for k in range(1, 2 * Z):
        push(red.at[dp], red.at[dp], d_s.at[k], d_r.at[k], {"dp": (dp + k) % (2 * Z), "expert": ex})
    for d in LATE[1::2]:
        put_grad(d)
    for j in range(BLOCKS // 2):
        tokens = pl.ds(j * 2 * TOK, 2 * TOK)
        grad = (raw[:, tokens] * wtok[:, tokens]).astype(BF16)
        hg_ref[0, :, pl.ds(j * TOK, TOK)] = lax.dot_general(grad, sel[j], NT, preferred_element_type=F32).astype(BF16)
    for k in range(1, 2 * Z):
        arrived(red.at[(dp - k + 2 * Z) % (2 * Z)], d_s.at[k], d_r.at[k])
    total = red[0]
    for k in range(1, 2 * Z):
        total = total + red[k]
    rt_ref[...] = total
    for op in sent:
        op.wait_send()


def body(out_grad, hidden, down_weight, experts, route_weight):
    vmem = pl.BlockSpec(memory_space=pltpu.VMEM)
    dma = pltpu.SemaphoreType.DMA
    hidden_grad, weight_grad, route = pl.pallas_call(
        kernel,
        out_shape=(
            jax.ShapeDtypeStruct((1, FFD, BLOCKS * MOST), BF16),
            jax.ShapeDtypeStruct(down_weight.shape, BF16),
            jax.ShapeDtypeStruct((4, TOK), F32),
        ),
        in_specs=[vmem] + [pl.BlockSpec(memory_space=pltpu.HBM)] * 4,
        out_specs=(vmem,) * 3,
        scratch_shapes=[
            pltpu.VMEM((1, FFD, BLOCKS * MOST), BF16),
            pltpu.VMEM(down_weight.shape, BF16),
            pltpu.VMEM((4, TOKENS), jnp.int32),
            pltpu.VMEM((4, TOKENS), F32),
            pltpu.VMEM((Z, 2, 4, 4, PIECE, TOK), BF16),
            pltpu.VMEM((FFD, TOKENS), F32),
            pltpu.VMEM((FFD, TOKENS), BF16),
            pltpu.VMEM((FFD, TOKENS), BF16),
            pltpu.VMEM((BLOCKS // 2, 2 * MOST, 2 * TOK), BF16),
            pltpu.VMEM((1, TOKENS), F32),
            pltpu.VMEM((BLOCKS, 8, TOK), F32),
            pltpu.VMEM((BLOCKS, 8, TOK), F32),
            pltpu.VMEM((2 * Z, 4, TOK), F32),
            dma((4,)),
            dma((3,)), dma((3,)),
            dma((8, 2, 4)), dma((8, 2, 4)),
            dma((5, 4, 2)), dma((5, 4, 2)),
            dma((2, 6)), dma((2, 6)),
            dma((GROUPS, 2)), dma((GROUPS, 2)),
            dma((GROUPS, 2)), dma((GROUPS, 2)),
            dma((GROUPS, 4)), dma((GROUPS, 4)),
            dma((BLOCKS,)), dma((BLOCKS,)),
            dma((2 * Z,)), dma((2 * Z,)),
        ],
        compiler_params=pltpu.CompilerParams(
            collective_id=0, has_side_effects=True, vmem_limit_bytes=42 << 20
        ),
        cost_estimate=pl.CostEstimate(flops=8 * 10**9, bytes_accessed=30 * 10**6, transcendentals=0),
        name="broadcast_grads",
    )(out_grad.T, hidden.swapaxes(1, 2), down_weight, experts.T, route_weight.T)
    return hidden_grad.swapaxes(1, 2), weight_grad, route.T


def solution(mesh):
    placed = (P("expert", "dp"), P("expert", None, "dp"), P("expert", "dp", None), P(), P())
    return jax.shard_map(
        body,
        mesh=mesh,
        in_specs=placed,
        out_specs=(P("expert", None, "dp"), P("expert", "dp", None), P("expert", None)),
        check_vma=False,
    )
```

```python
import functools

import jax
import jax.numpy as jnp
from jax import lax
from jax.experimental import pallas as pl
from jax.experimental.pallas import tpu as pltpu
from jax.sharding import PartitionSpec as P

MESH = pl.DeviceIdType.MESH
F32, BF16 = jnp.float32, jnp.bfloat16

Z = 16
PIECE = 192
FEAT = 384
BLOCKS = 16
TOK = 128
TOKENS = BLOCKS * TOK
FFD = 168
MOST = 64
GROUPS = 9
NT = (((1,), (1,)), ((), ()))
ORDER = (0, 1, 3, 2)
EARLY = (0, 1, 2, 3)
EARLY_SLOTS = (0, 1, 2, 3, 4, 5, 6)
SKIP = 5
LATE = (5, 7, 8)

PLAN = (
    "U1", "U3", "Z10", "U2", "Z11", "Z13", "P0", "Z12", "Z20", "Z21", "Z23", "L0", "Z22", "P1", "Z30", "Z31", "Z33",
    "R0", "Z32", "P2", "Z40", "L1", "G0", "Z41", "Z43", "Z42", "R1", "Z50", "P3", "Z51", "Z53", "L2", "G1", "Z52",
    "Z60", "R2", "Z61", "P4", "Z63", "G2", "Z62", "L3", "Z70", "E0", "Z71", "E1", "Z73", "L4", "R3", "Z72", "G3", "Z80",
    "R4", "E2", "G4", "P6", "Z81", "F0", "E3", "Z83", "F1", "Z82", "E4", "P7", "F2", "E5", "L6", "F3", "P8", "R6", "F4",
    "G6", "L7", "F5", "L8", "R7", "R5", "R8",
)


def kernel(
    og_ref, hid_hbm, w_hbm, ex_hbm, rw_hbm,
    hg_ref, wg_ref, rt_ref,
    hid_ref, w_ref, ex_ref, rw_ref,
    rows, raw, ht, hw, sel, wtok, sg, sgx, red,
    load, u_s, u_r, z_s, z_r, p_s, p_r, e_s, e_r, v_s, v_r, a_s, a_r, c_s, c_r, x_s, x_r, d_s, d_r,
):
    dp, ex = lax.axis_index("dp"), lax.axis_index("expert")
    z, ylo = dp // 2, dp % 2
    x, yhi, c = ex // 4, (ex // 2) % 2, ex % 2
    y = yhi * 2 + ylo
    u = y + c * (x - y)
    v = x + c * (y - x)

    def at(x, y, z, c):
        return {"dp": z * 2 + y % 2, "expert": (x * 2 + y // 2) * 2 + c}

    def along(du, dv):
        uu, vv = (u + du + 4) % 4, (v + dv + 4) % 4
        return at(vv + c * (uu - vv), uu + c * (vv - uu), z, c)

    def beside(dz):
        return at(x, y, (z + dz + Z) % Z, c)

    twin = at(x, y, z, 1 - c)

    loads = [
        pltpu.make_async_copy(src, dst, load.at[i])
        for i, (src, dst) in enumerate(
            ((ex_hbm, ex_ref), (rw_hbm, rw_ref), (hid_hbm, hid_ref), (w_hbm, w_ref))
        )
    ]
    loads.append(pltpu.make_async_copy(og_ref, rows.at[0, c, v, u], load.at[4]))
    for op in loads:
        op.start()

    barrier = pltpu.get_barrier_semaphore()
    greeted = [along(k, 0) for k in (1, 2, 3)] + [along(0, k) for k in (1, 3)]
    greeted += [beside(1), beside(-1), twin]
    for device in greeted:
        pl.semaphore_signal(barrier, inc=1, device_id=device, device_id_type=MESH)
    pl.semaphore_wait(barrier, len(greeted))

    sent = []

    def copy(src, dst, send, recv, device):
        return pltpu.make_async_remote_copy(
            src_ref=src, dst_ref=dst, send_sem=send, recv_sem=recv, device_id=device, device_id_type=MESH
        )

    def push(src, dst, send, recv, device):
        op = copy(src, dst, send, recv, device)
        op.start()
        sent.append(op)

    def arrived(dst, send, recv):
        copy(dst, dst, send, recv, twin).wait_recv()


    def piece(slot, vv, k):
        return rows.at[slot, c, vv, (u - k + 4) % 4]

    def z_send(d, k):
        for way in (0, 1):
            if d == 7 and way != k // 2:
                continue
            src = 0 if d == 0 else 2 * d - 1 + way
            dst = 15 if d == 7 else 2 * d + 1 + way
            own = og_ref if d == 0 and k == 0 else piece(src, v, k)
            push(own, piece(dst, v, k), z_s.at[d, way, k], z_r.at[d, way, k], beside(1 - 2 * way))

    def z_wait(d, k):
        for way in (0, 1):
            if d == 8 and way != k // 2:
                continue
            dst = 15 if d == 8 else 2 * d - 1 + way
            arrived(piece(dst, v, k), z_s.at[d - 1, way, k], z_r.at[d - 1, way, k])

    def slot_list(d):
        return (0,) if d == 0 else (15,) if d == 8 else (2 * d - 1, 2 * d)

    def slots(d):
        return pl.ds(0, 1) if d == 0 else pl.ds(15, 1) if d == 8 else pl.ds(2 * d - 1, 2)

    def v_all(d, vv):
        return rows.at[slots(d), c, vv]

    def v_half(d, vv, way):
        if d in (0, 8):
            return rows.at[slots(d), c, vv, pl.ds(2 * way, 2)]
        return rows.at[pl.ds(2 * d - 1 + way, 1), c, vv]

    def v_send(d):
        for way in (0, 1):
            own = v_all(d, v)
            push(own, own, v_s.at[d, way], v_r.at[d, way], along(0, 1 - 2 * way))

    def v_piece(slot, k):
        at_slot = EARLY_SLOTS.index(slot)
        for way in (0, 1):
            own = og_ref if slot == 0 and k == 0 else piece(slot, v, k)
            push(own, piece(slot, v, k), p_s.at[at_slot, k, way], p_r.at[at_slot, k, way], along(0, 1 - 2 * way))

    def v_pass(d):
        for way in (0, 1):
            step = 1 - 2 * way
            vv = (v - step + 4) % 4
            if d in EARLY:
                for slot in slot_list(d):
                    for k in ORDER:
                        at_slot = EARLY_SLOTS.index(slot)
                        arrived(piece(slot, vv, k), p_s.at[at_slot, k, way], p_r.at[at_slot, k, way])
            else:
                arrived(v_all(d, vv), v_s.at[d, way], v_r.at[d, way])
            half = v_half(d, vv, way)
            push(half, half, a_s.at[d, way], a_r.at[d, way], along(0, step))

    def v_last(d):
        for way in (0, 1):
            arrived(v_half(d, (v + 2) % 4, way), a_s.at[d, way], a_r.at[d, way])

    def e_part(slot, unit):
        return rows.at[slot, c, (v + (1, 3, 2)[unit // 2]) % 4, pl.ds(2 * (unit % 2), 2)]

    def e_send(unit):
        for way in (0, 1):
            src, dst = e_part(2 * SKIP - 3 + way, unit), e_part(2 * SKIP - 1 + way, unit)
            push(src, dst, e_s.at[way, unit], e_r.at[way, unit], beside(1 - 2 * way))

    def e_wait(unit):
        for way in (0, 1):
            arrived(e_part(2 * SKIP - 1 + way, unit), e_s.at[way, unit], e_r.at[way, unit])

    def c_send(d, k):
        own = rows.at[slots(d), c, (v + k) % 4]
        push(own, own, c_s.at[d, k], c_r.at[d, k], twin)

    def c_wait(d):
        for k in range(4):
            arrived(rows.at[slots(d), 1 - c, (u + k) % 4], c_s.at[d, k], c_r.at[d, k])

    def prepare():
        mine = ex_ref[...] == ex
        hit = jnp.max(jnp.where(mine, 1.0, 0.0), axis=0, keepdims=True)
        wtok[...] = jnp.sum(jnp.where(mine, rw_ref[...], 0.0), axis=0, keepdims=True)
        hits = jnp.concatenate([hit[:, b * TOK : (b + 1) * TOK] for b in range(BLOCKS)], axis=0)
        upto = lax.broadcasted_iota(jnp.int32, (TOK, TOK), 0) <= lax.broadcasted_iota(jnp.int32, (TOK, TOK), 1)
        count = jnp.dot(hits.astype(BF16), jnp.where(upto, 1.0, 0.0).astype(BF16), preferred_element_type=F32)
        code = jnp.where(hits > 0, count - 1.0, -1000.0)
        slot = lax.broadcasted_iota(jnp.int32, (2 * MOST, 2 * TOK), 0).astype(F32)
        for j in range(BLOCKS // 2):
            both = jnp.concatenate([code[2 * j : 2 * j + 1], code[2 * j + 1 : 2 * j + 2] + float(MOST)], axis=1)
            one = jnp.where(slot == both, 1.0, 0.0).astype(BF16)
            sel[j] = one
            tokens = pl.ds(j * 2 * TOK, 2 * TOK)
            part = jnp.dot(hid_ref[0, :, pl.ds(j * TOK, TOK)], one, preferred_element_type=F32)
            ht[:, tokens] = part.astype(BF16)
            hw[:, tokens] = (part * wtok[:, tokens]).astype(BF16)

    def places(d):
        if d == 0:
            return ((0, z),)
        if d == 8:
            return ((15, (z + 8) % Z),)
        return ((2 * d - 1, (z - d + Z) % Z), (2 * d, (z + d) % Z))

    def columns(zi):
        return pl.ds(pl.multiple_of(zi * FEAT, 128), FEAT)

    def block(s, xx, yh, core):
        if core == 0:
            return rows[s, 0, xx, 2 * yh : 2 * yh + 2].reshape(FEAT, TOK)
        return jnp.concatenate([rows[s, 1, 2 * yh, xx], rows[s, 1, 2 * yh + 1, xx]], axis=0)

    def slab(s, xx):
        return jnp.concatenate([block(s, xx, b // 2, b % 2) for b in range(4)], axis=1)

    def add_raw(d, first):
        here = places(d)
        w = jnp.concatenate([w_ref[0, :, columns(zi)] for _, zi in here], axis=1)

        for xx in range(4):
            t = jnp.concatenate([slab(s, xx) for s, _ in here], axis=0)
            tokens = pl.ds(xx * 4 * TOK, 4 * TOK)
            more = jnp.dot(w, t, preferred_element_type=F32)
            raw[:, tokens] = more if first else raw[:, tokens] + more

    def add_last(core):
        w = w_ref[0, :, columns((z + 8) % Z)]

        for xx in range(4):
            t = jnp.concatenate([block(15, xx, yh, core) for yh in (0, 1)], axis=1)
            more = jnp.dot(w, t, preferred_element_type=F32)
            for yh in (0, 1):
                tokens = pl.ds((4 * xx + 2 * yh + core) * TOK, TOK)
                raw[:, tokens] += more[:, yh * TOK : (yh + 1) * TOK]

    def put_grad(d):
        here = places(d)
        t = jnp.concatenate(
            [jnp.concatenate([slab(s, xx) for xx in range(4)], axis=1) for s, _ in here], axis=0
        )
        grad = lax.dot_general(hw[...], t, NT, preferred_element_type=F32).astype(BF16)
        for i, (_, zi) in enumerate(here):
            wg_ref[0, :, columns(zi)] = grad[:, i * FEAT : (i + 1) * FEAT]

    for k in (1, 3, 2):
        push(og_ref, piece(0, v, 0), u_s.at[k - 1], u_r.at[k - 1], along(k, 0))
    z_send(0, 0)
    v_piece(0, 0)
    for op in loads[:3]:
        op.wait()
    prepare()
    for op in loads[3:]:
        op.wait()

    def on_u(k):
        arrived(piece(0, v, k), u_s.at[k - 1], u_r.at[k - 1])
        z_send(0, k)
        v_piece(0, k)
        if k == ORDER[3]:
            c_send(0, 0)

    def on_z(d, k):
        z_wait(d, k)
        if d < 8:
            z_send(d, k)
        if d in EARLY:
            for slot in slot_list(d):
                v_piece(slot, k)
        if k == ORDER[3]:
            if d not in EARLY and d != SKIP:
                v_send(d)
            c_send(d, 0)

    def on_v(d):
        v_pass(d)
        c_send(d, 1)
        c_send(d, 3)

    def on_far(d):
        v_last(d)
        c_send(d, 2)

    def on_e(unit):
        e_wait(unit)
        if unit % 2 == 1:
            c_send(SKIP, (1, 3, 2)[unit // 2])

    summed = []
    for step in PLAN:
        kind, d = step[0], int(step[1])
        if kind == "U":
            on_u(d)
        elif kind == "Z":
            on_z(d, int(step[2]))
        elif kind == "P":
            on_v(d)
        elif kind == "L":
            on_far(d)
        elif kind == "E":
            e_send(d)
        elif kind == "F":
            on_e(d)
        elif kind == "R" and d == 8:
            continue
        elif kind == "R":
            c_wait(d)
            add_raw(d, not summed)
            summed.append(d)
        else:
            put_grad(d)

    def tell(core, first):
        for i in range(BLOCKS // 2):
            b = 2 * i + core
            tokens = pl.ds(pl.multiple_of(b * TOK, TOK), TOK)
            share = jnp.sum(ht[:, tokens].astype(F32) * raw[:, tokens], axis=0, keepdims=True)
            sg[b] = jnp.broadcast_to(share, (8, TOK))
        for k in range(first, BLOCKS, 2):
            to = (ex + k) % BLOCKS
            push(sg.at[to], sgx.at[ex], x_s.at[k], x_r.at[k], {"dp": dp, "expert": to})

    for core in (0, 1):
        pl.when(c == core)(functools.partial(add_last, core))
    tell(c, 2)
    c_wait(8)
    for core in (0, 1):
        pl.when(c != core)(functools.partial(add_last, core))
    tell(1 - c, 1)
    sgx[ex] = sg[ex]
    for d in LATE[::2]:
        put_grad(d)
    named = ex_ref[:, pl.ds(pl.multiple_of(ex * TOK, TOK), TOK)]
    total = jnp.zeros((4, TOK), F32)
    for k in range(1, BLOCKS):
        arrived(sgx.at[(ex - k + BLOCKS) % BLOCKS], x_s.at[k], x_r.at[k])
    for e in range(BLOCKS):
        total = total + jnp.where(named == e, sgx[e, 0:1, :], 0.0)
    red[dp] = total
    before = len(sent)
    for k in sorted(range(1, 2 * Z), key=lambda k: -min(k, 2 * Z - k)):
        push(red.at[dp], red.at[dp], d_s.at[k], d_r.at[k], {"dp": (dp + k) % (2 * Z), "expert": ex})
    for d in LATE[1::2]:
        put_grad(d)
    for j in range(BLOCKS // 2):
        tokens = pl.ds(j * 2 * TOK, 2 * TOK)
        grad = (raw[:, tokens] * wtok[:, tokens]).astype(BF16)
        hg_ref[0, :, pl.ds(j * TOK, TOK)] = lax.dot_general(grad, sel[j], NT, preferred_element_type=F32).astype(BF16)
    for op in sent[:before]:
        op.wait_send()
    for k in range(1, 2 * Z):
        arrived(red.at[(dp - k + 2 * Z) % (2 * Z)], d_s.at[k], d_r.at[k])
    total = red[0]
    for k in range(1, 2 * Z):
        total = total + red[k]
    rt_ref[...] = total
    for op in sent[before:]:
        op.wait_send()


def body(out_grad, hidden, down_weight, experts, route_weight):
    vmem = pl.BlockSpec(memory_space=pltpu.VMEM)
    dma = pltpu.SemaphoreType.DMA
    operands = (out_grad.T, hidden.swapaxes(1, 2), down_weight, experts.T, route_weight.T)
    hidden_grad, weight_grad, route = pl.pallas_call(
        kernel,
        out_shape=(
            jax.ShapeDtypeStruct((1, FFD, BLOCKS * MOST), BF16),
            jax.ShapeDtypeStruct(down_weight.shape, BF16),
            jax.ShapeDtypeStruct((4, TOK), F32),
        ),
        in_specs=[pl.BlockSpec(memory_space=pltpu.HBM)] * 5,
        out_specs=(vmem,) * 3,
        scratch_shapes=[
            pltpu.VMEM((1, FFD, BLOCKS * MOST), BF16),
            pltpu.VMEM(down_weight.shape, BF16),
            pltpu.VMEM((4, TOKENS), jnp.int32),
            pltpu.VMEM((4, TOKENS), F32),
            pltpu.VMEM((Z, 2, 4, 4, PIECE, TOK), BF16),
            pltpu.VMEM((FFD, TOKENS), F32),
            pltpu.VMEM((FFD, TOKENS), BF16),
            pltpu.VMEM((FFD, TOKENS), BF16),
            pltpu.VMEM((BLOCKS // 2, 2 * MOST, 2 * TOK), BF16),
            pltpu.VMEM((1, TOKENS), F32),
            pltpu.VMEM((BLOCKS, 8, TOK), F32),
            pltpu.VMEM((BLOCKS, 8, TOK), F32),
            pltpu.VMEM((2 * Z, 4, TOK), F32),
            dma((5,)),
            dma((3,)), dma((3,)),
            dma((8, 2, 4)), dma((8, 2, 4)),
            dma((7, 4, 2)), dma((7, 4, 2)),
            dma((2, 6)), dma((2, 6)),
            dma((GROUPS, 2)), dma((GROUPS, 2)),
            dma((GROUPS, 2)), dma((GROUPS, 2)),
            dma((GROUPS, 4)), dma((GROUPS, 4)),
            dma((BLOCKS,)), dma((BLOCKS,)),
            dma((2 * Z,)), dma((2 * Z,)),
        ],
        compiler_params=pltpu.CompilerParams(
            collective_id=0, has_side_effects=True, vmem_limit_bytes=42 << 20
        ),
        cost_estimate=pl.CostEstimate(flops=8 * 10**9, bytes_accessed=30 * 10**6, transcendentals=0),
        name="broadcast_grads",
    )(*(pltpu.with_memory_space_constraint(a, pltpu.HBM) for a in operands))
    return hidden_grad.swapaxes(1, 2), weight_grad, route.T


def solution(mesh):
    placed = (P("expert", "dp"), P("expert", None, "dp"), P("expert", "dp", None), P(), P())
    return jax.shard_map(
        body,
        mesh=mesh,
        in_specs=placed,
        out_specs=(P("expert", None, "dp"), P("expert", "dp", None), P("expert", None)),
        check_vma=False,
    )
```

```python
import functools

import jax
import jax.numpy as jnp
from jax import lax
from jax.experimental import pallas as pl
from jax.experimental.pallas import tpu as pltpu
from jax.sharding import PartitionSpec as P

MESH = pl.DeviceIdType.MESH
F32, BF16 = jnp.float32, jnp.bfloat16

Z = 16
PIECE = 192
FEAT = 384
BLOCKS = 16
TOK = 128
TOKENS = BLOCKS * TOK
FFD = 168
MOST = 64
GROUPS = 9
NT = (((1,), (1,)), ((), ()))
ORDER = (0, 1, 3, 2)
EARLY = (0, 1, 2, 3)
EARLY_SLOTS = (0, 1, 2, 3, 4, 5, 6)
SKIP = 5
LATE = (5, 7, 8)

PLAN = (
    "U1", "U3", "Z10", "U2", "Z11", "Z13", "P0", "Z12", "Z20", "Z21", "Z23", "L0", "Z22", "P1", "Z30", "Z31", "Z33",
    "R0", "Z32", "P2", "Z40", "L1", "G0", "Z41", "Z43", "Z42", "R1", "Z50", "P3", "Z51", "Z53", "L2", "G1", "Z52",
    "Z60", "R2", "Z61", "P4", "Z63", "G2", "Z62", "L3", "Z70", "E0", "Z71", "E1", "Z73", "L4", "R3", "Z72", "G3", "Z80",
    "R4", "E2", "G4", "P6", "Z81", "F0", "E3", "Z83", "F1", "Z82", "E4", "P7", "F2", "E5", "L6", "F3", "P8", "R6", "F4",
    "G6", "L7", "F5", "L8", "R7", "R5", "R8",
)


def kernel(
    og_ref, hid_hbm, w_hbm, ex_hbm, rw_hbm,
    hg_ref, wg_ref, rt_ref,
    hid_ref, w_ref, ex_ref, rw_ref,
    rows, raw, ht, hw, sel, wtok, sg, sgx, red,
    load, u_s, u_r, z_s, z_r, p_s, p_r, e_s, e_r, v_s, v_r, a_s, a_r, c_s, c_r, x_s, x_r, d_s, d_r,
):
    dp, ex = lax.axis_index("dp"), lax.axis_index("expert")
    z, ylo = dp // 2, dp % 2
    x, yhi, c = ex // 4, (ex // 2) % 2, ex % 2
    y = yhi * 2 + ylo
    u = y + c * (x - y)
    v = x + c * (y - x)

    def at(x, y, z, c):
        return {"dp": z * 2 + y % 2, "expert": (x * 2 + y // 2) * 2 + c}

    def along(du, dv):
        uu, vv = (u + du + 4) % 4, (v + dv + 4) % 4
        return at(vv + c * (uu - vv), uu + c * (vv - uu), z, c)

    def beside(dz):
        return at(x, y, (z + dz + Z) % Z, c)

    twin = at(x, y, z, 1 - c)

    barrier = pltpu.get_barrier_semaphore()
    greeted = [along(k, 0) for k in (1, 2, 3)] + [along(0, k) for k in (1, 3)]
    greeted += [beside(1), beside(-1), twin]
    for device in greeted:
        pl.semaphore_signal(barrier, inc=1, device_id=device, device_id_type=MESH)
    loads = [
        pltpu.make_async_copy(src, dst, load.at[i])
        for i, (src, dst) in enumerate(
            ((ex_hbm, ex_ref), (rw_hbm, rw_ref), (hid_hbm, hid_ref), (w_hbm, w_ref))
        )
    ]
    loads.append(pltpu.make_async_copy(og_ref, rows.at[0, c, v, u], load.at[4]))
    for op in loads:
        op.start()
    pl.semaphore_wait(barrier, len(greeted))
    loads[4].wait()

    sent = []

    def copy(src, dst, send, recv, device):
        return pltpu.make_async_remote_copy(
            src_ref=src, dst_ref=dst, send_sem=send, recv_sem=recv, device_id=device, device_id_type=MESH
        )

    def push(src, dst, send, recv, device):
        op = copy(src, dst, send, recv, device)
        op.start()
        sent.append(op)

    def arrived(dst, send, recv):
        copy(dst, dst, send, recv, twin).wait_recv()


    def piece(slot, vv, k):
        return rows.at[slot, c, vv, (u - k + 4) % 4]

    def z_send(d, k):
        for way in (0, 1):
            if d == 7 and way != k // 2:
                continue
            src = 0 if d == 0 else 2 * d - 1 + way
            dst = 15 if d == 7 else 2 * d + 1 + way
            push(piece(src, v, k), piece(dst, v, k), z_s.at[d, way, k], z_r.at[d, way, k], beside(1 - 2 * way))

    def z_wait(d, k):
        for way in (0, 1):
            if d == 8 and way != k // 2:
                continue
            dst = 15 if d == 8 else 2 * d - 1 + way
            arrived(piece(dst, v, k), z_s.at[d - 1, way, k], z_r.at[d - 1, way, k])

    def slot_list(d):
        return (0,) if d == 0 else (15,) if d == 8 else (2 * d - 1, 2 * d)

    def slots(d):
        return pl.ds(0, 1) if d == 0 else pl.ds(15, 1) if d == 8 else pl.ds(2 * d - 1, 2)

    def v_all(d, vv):
        return rows.at[slots(d), c, vv]

    def v_half(d, vv, way):
        if d in (0, 8):
            return rows.at[slots(d), c, vv, pl.ds(2 * way, 2)]
        return rows.at[pl.ds(2 * d - 1 + way, 1), c, vv]

    def v_send(d):
        for way in (0, 1):
            own = v_all(d, v)
            push(own, own, v_s.at[d, way], v_r.at[d, way], along(0, 1 - 2 * way))

    def v_piece(slot, k):
        at_slot = EARLY_SLOTS.index(slot)
        for way in (0, 1):
            push(piece(slot, v, k), piece(slot, v, k), p_s.at[at_slot, k, way], p_r.at[at_slot, k, way], along(0, 1 - 2 * way))

    def v_pass(d):
        for way in (0, 1):
            step = 1 - 2 * way
            vv = (v - step + 4) % 4
            if d in EARLY:
                for slot in slot_list(d):
                    for k in ORDER:
                        at_slot = EARLY_SLOTS.index(slot)
                        arrived(piece(slot, vv, k), p_s.at[at_slot, k, way], p_r.at[at_slot, k, way])
            else:
                arrived(v_all(d, vv), v_s.at[d, way], v_r.at[d, way])
            half = v_half(d, vv, way)
            push(half, half, a_s.at[d, way], a_r.at[d, way], along(0, step))

    def v_last(d):
        for way in (0, 1):
            arrived(v_half(d, (v + 2) % 4, way), a_s.at[d, way], a_r.at[d, way])

    def e_part(slot, unit):
        return rows.at[slot, c, (v + (1, 3, 2)[unit // 2]) % 4, pl.ds(2 * (unit % 2), 2)]

    def e_send(unit):
        for way in (0, 1):
            src, dst = e_part(2 * SKIP - 3 + way, unit), e_part(2 * SKIP - 1 + way, unit)
            push(src, dst, e_s.at[way, unit], e_r.at[way, unit], beside(1 - 2 * way))

    def e_wait(unit):
        for way in (0, 1):
            arrived(e_part(2 * SKIP - 1 + way, unit), e_s.at[way, unit], e_r.at[way, unit])

    def c_send(d, k):
        own = rows.at[slots(d), c, (v + k) % 4]
        push(own, own, c_s.at[d, k], c_r.at[d, k], twin)

    def c_wait(d):
        for k in range(4):
            arrived(rows.at[slots(d), 1 - c, (u + k) % 4], c_s.at[d, k], c_r.at[d, k])

    def prepare():
        mine = ex_ref[...] == ex
        hit = jnp.max(jnp.where(mine, 1.0, 0.0), axis=0, keepdims=True)
        wtok[...] = jnp.sum(jnp.where(mine, rw_ref[...], 0.0), axis=0, keepdims=True)
        hits = jnp.concatenate([hit[:, b * TOK : (b + 1) * TOK] for b in range(BLOCKS)], axis=0)
        upto = lax.broadcasted_iota(jnp.int32, (TOK, TOK), 0) <= lax.broadcasted_iota(jnp.int32, (TOK, TOK), 1)
        count = jnp.dot(hits.astype(BF16), jnp.where(upto, 1.0, 0.0).astype(BF16), preferred_element_type=F32)
        code = jnp.where(hits > 0, count - 1.0, -1000.0)
        slot = lax.broadcasted_iota(jnp.int32, (2 * MOST, 2 * TOK), 0).astype(F32)
        for j in range(BLOCKS // 2):
            both = jnp.concatenate([code[2 * j : 2 * j + 1], code[2 * j + 1 : 2 * j + 2] + float(MOST)], axis=1)
            one = jnp.where(slot == both, 1.0, 0.0).astype(BF16)
            sel[j] = one
            tokens = pl.ds(j * 2 * TOK, 2 * TOK)
            part = jnp.dot(hid_ref[0, :, pl.ds(j * TOK, TOK)], one, preferred_element_type=F32)
            ht[:, tokens] = part.astype(BF16)
            hw[:, tokens] = (part * wtok[:, tokens]).astype(BF16)

    def places(d):
        if d == 0:
            return ((0, z),)
        if d == 8:
            return ((15, (z + 8) % Z),)
        return ((2 * d - 1, (z - d + Z) % Z), (2 * d, (z + d) % Z))

    def columns(zi):
        return pl.ds(pl.multiple_of(zi * FEAT, 128), FEAT)

    def block(s, xx, yh, core):
        if core == 0:
            return rows[s, 0, xx, 2 * yh : 2 * yh + 2].reshape(FEAT, TOK)
        return jnp.concatenate([rows[s, 1, 2 * yh, xx], rows[s, 1, 2 * yh + 1, xx]], axis=0)

    def slab(s, xx):
        return jnp.concatenate([block(s, xx, b // 2, b % 2) for b in range(4)], axis=1)

    def add_raw(d, first):
        here = places(d)
        w = jnp.concatenate([w_ref[0, :, columns(zi)] for _, zi in here], axis=1)

        for xx in range(4):
            t = jnp.concatenate([slab(s, xx) for s, _ in here], axis=0)
            tokens = pl.ds(xx * 4 * TOK, 4 * TOK)
            more = jnp.dot(w, t, preferred_element_type=F32)
            raw[:, tokens] = more if first else raw[:, tokens] + more

    def add_last(core):
        w = w_ref[0, :, columns((z + 8) % Z)]

        for xx in range(4):
            t = jnp.concatenate([block(15, xx, yh, core) for yh in (0, 1)], axis=1)
            more = jnp.dot(w, t, preferred_element_type=F32)
            for yh in (0, 1):
                tokens = pl.ds((4 * xx + 2 * yh + core) * TOK, TOK)
                raw[:, tokens] += more[:, yh * TOK : (yh + 1) * TOK]

    def put_grad(d):
        here = places(d)
        t = jnp.concatenate(
            [jnp.concatenate([slab(s, xx) for xx in range(4)], axis=1) for s, _ in here], axis=0
        )
        grad = lax.dot_general(hw[...], t, NT, preferred_element_type=F32).astype(BF16)
        for i, (_, zi) in enumerate(here):
            wg_ref[0, :, columns(zi)] = grad[:, i * FEAT : (i + 1) * FEAT]

    for k in (1, 3, 2):
        push(piece(0, v, 0), piece(0, v, 0), u_s.at[k - 1], u_r.at[k - 1], along(k, 0))
    z_send(0, 0)
    v_piece(0, 0)
    for op in loads[:3]:
        op.wait()
    prepare()
    loads[3].wait()

    def on_u(k):
        arrived(piece(0, v, k), u_s.at[k - 1], u_r.at[k - 1])
        z_send(0, k)
        v_piece(0, k)
        if k == ORDER[3]:
            c_send(0, 0)

    def on_z(d, k):
        z_wait(d, k)
        if d < 8:
            z_send(d, k)
        if d in EARLY:
            for slot in slot_list(d):
                v_piece(slot, k)
        if k == ORDER[3]:
            if d not in EARLY and d != SKIP:
                v_send(d)
            c_send(d, 0)

    def on_v(d):
        v_pass(d)
        c_send(d, 1)
        c_send(d, 3)

    def on_far(d):
        v_last(d)
        c_send(d, 2)

    def on_e(unit):
        e_wait(unit)
        if unit % 2 == 1:
            c_send(SKIP, (1, 3, 2)[unit // 2])

    summed = []
    for step in PLAN:
        kind, d = step[0], int(step[1])
        if kind == "U":
            on_u(d)
        elif kind == "Z":
            on_z(d, int(step[2]))
        elif kind == "P":
            on_v(d)
        elif kind == "L":
            on_far(d)
        elif kind == "E":
            e_send(d)
        elif kind == "F":
            on_e(d)
        elif kind == "R" and d == 8:
            continue
        elif kind == "R":
            c_wait(d)
            add_raw(d, not summed)
            summed.append(d)
        else:
            put_grad(d)

    def tell(core, first):
        for i in range(BLOCKS // 2):
            b = 2 * i + core
            tokens = pl.ds(pl.multiple_of(b * TOK, TOK), TOK)
            share = jnp.sum(ht[:, tokens].astype(F32) * raw[:, tokens], axis=0, keepdims=True)
            sg[b] = jnp.broadcast_to(share, (8, TOK))
        for k in range(first, BLOCKS, 2):
            to = (ex + k) % BLOCKS
            push(sg.at[to], sgx.at[ex], x_s.at[k], x_r.at[k], {"dp": dp, "expert": to})

    for core in (0, 1):
        pl.when(c == core)(functools.partial(add_last, core))
    tell(c, 2)
    c_wait(8)
    for core in (0, 1):
        pl.when(c != core)(functools.partial(add_last, core))
    tell(1 - c, 1)
    sgx[ex] = sg[ex]
    for d in LATE[::2]:
        put_grad(d)
    named = ex_ref[:, pl.ds(pl.multiple_of(ex * TOK, TOK), TOK)]
    total = jnp.zeros((4, TOK), F32)
    for k in range(1, BLOCKS):
        arrived(sgx.at[(ex - k + BLOCKS) % BLOCKS], x_s.at[k], x_r.at[k])
    for e in range(BLOCKS):
        total = total + jnp.where(named == e, sgx[e, 0:1, :], 0.0)
    red[dp] = total
    before = len(sent)
    for k in sorted(range(1, 2 * Z), key=lambda k: -min(k, 2 * Z - k)):
        push(red.at[dp], red.at[dp], d_s.at[k], d_r.at[k], {"dp": (dp + k) % (2 * Z), "expert": ex})
    for d in LATE[1::2]:
        put_grad(d)
    for j in range(BLOCKS // 2):
        tokens = pl.ds(j * 2 * TOK, 2 * TOK)
        grad = (raw[:, tokens] * wtok[:, tokens]).astype(BF16)
        hg_ref[0, :, pl.ds(j * TOK, TOK)] = lax.dot_general(grad, sel[j], NT, preferred_element_type=F32).astype(BF16)
    for op in sent[:before]:
        op.wait_send()
    for k in range(1, 2 * Z):
        arrived(red.at[(dp - k + 2 * Z) % (2 * Z)], d_s.at[k], d_r.at[k])
    total = red[0]
    for k in range(1, 2 * Z):
        total = total + red[k]
    rt_ref[...] = total
    for op in sent[before:]:
        op.wait_send()


def hand_over(hg_ref, wg_ref, rt_ref, hg_out, wg_out, rt_out, sems):
    width = wg_ref.shape[2] // 4
    copies = [(wg_ref.at[:, :, pl.ds(i * width, width)], wg_out.at[:, :, pl.ds(i * width, width)]) for i in range(4)]
    copies += [(hg_ref, hg_out), (rt_ref, rt_out)]
    copies = [pltpu.make_async_copy(src, dst, sems.at[i]) for i, (src, dst) in enumerate(copies)]
    for op in copies:
        op.start()
    for op in copies:
        op.wait()


def body(out_grad, hidden, down_weight, experts, route_weight):
    vmem = pl.BlockSpec(memory_space=pltpu.VMEM)
    dma = pltpu.SemaphoreType.DMA
    operands = (out_grad.T, hidden.swapaxes(1, 2), down_weight, experts.T, route_weight.T)
    shapes = (
        jax.ShapeDtypeStruct((1, FFD, BLOCKS * MOST), BF16),
        jax.ShapeDtypeStruct(down_weight.shape, BF16),
        jax.ShapeDtypeStruct((4, TOK), F32),
    )
    results = pl.pallas_call(
        kernel,
        out_shape=shapes,
        in_specs=[pl.BlockSpec(memory_space=pltpu.HBM)] * 5,
        out_specs=(vmem,) * 3,
        scratch_shapes=[
            pltpu.VMEM((1, FFD, BLOCKS * MOST), BF16),
            pltpu.VMEM(down_weight.shape, BF16),
            pltpu.VMEM((4, TOKENS), jnp.int32),
            pltpu.VMEM((4, TOKENS), F32),
            pltpu.VMEM((Z, 2, 4, 4, PIECE, TOK), BF16),
            pltpu.VMEM((FFD, TOKENS), F32),
            pltpu.VMEM((FFD, TOKENS), BF16),
            pltpu.VMEM((FFD, TOKENS), BF16),
            pltpu.VMEM((BLOCKS // 2, 2 * MOST, 2 * TOK), BF16),
            pltpu.VMEM((1, TOKENS), F32),
            pltpu.VMEM((BLOCKS, 8, TOK), F32),
            pltpu.VMEM((BLOCKS, 8, TOK), F32),
            pltpu.VMEM((2 * Z, 4, TOK), F32),
            dma((5,)),
            dma((3,)), dma((3,)),
            dma((8, 2, 4)), dma((8, 2, 4)),
            dma((7, 4, 2)), dma((7, 4, 2)),
            dma((2, 6)), dma((2, 6)),
            dma((GROUPS, 2)), dma((GROUPS, 2)),
            dma((GROUPS, 2)), dma((GROUPS, 2)),
            dma((GROUPS, 4)), dma((GROUPS, 4)),
            dma((BLOCKS,)), dma((BLOCKS,)),
            dma((2 * Z,)), dma((2 * Z,)),
        ],
        compiler_params=pltpu.CompilerParams(
            collective_id=0, has_side_effects=True, vmem_limit_bytes=42 << 20
        ),
        cost_estimate=pl.CostEstimate(flops=8 * 10**9, bytes_accessed=30 * 10**6, transcendentals=0),
        name="broadcast_grads",
    )(*(pltpu.with_memory_space_constraint(a, pltpu.HBM) for a in operands))
    hidden_grad, weight_grad, route = pl.pallas_call(
        hand_over,
        out_shape=shapes,
        in_specs=[pl.BlockSpec(memory_space=pl.ANY)] * 3,
        out_specs=(pl.BlockSpec(memory_space=pltpu.HBM),) * 3,
        scratch_shapes=[dma((6,))],
        compiler_params=pltpu.CompilerParams(vmem_limit_bytes=1 << 20),
        name="hand_over",
    )(*results)
    return hidden_grad.swapaxes(1, 2), weight_grad, route.T


def solution(mesh):
    placed = (P("expert", "dp"), P("expert", None, "dp"), P("expert", "dp", None), P(), P())
    return jax.shard_map(
        body,
        mesh=mesh,
        in_specs=placed,
        out_specs=(P("expert", None, "dp"), P("expert", "dp", None), P("expert", None)),
        check_vma=False,
    )
```

```python
import functools

import jax
import jax.numpy as jnp
from jax import lax
from jax.experimental import pallas as pl
from jax.experimental.pallas import tpu as pltpu
from jax.sharding import PartitionSpec as P

MESH = pl.DeviceIdType.MESH
F32, BF16 = jnp.float32, jnp.bfloat16

Z = 16
PIECE = 192
FEAT = 384
BLOCKS = 16
TOK = 128
TOKENS = BLOCKS * TOK
FFD = 168
MOST = 64
GROUPS = 9
NT = (((1,), (1,)), ((), ()))
ORDER = (0, 1, 3, 2)
EARLY = (0, 1, 2, 3)
EARLY_SLOTS = (0, 1, 2, 3, 4, 5, 6)
SKIP = 5
LATE = (5, 7, 8)

PLAN = (
    "U1", "U3", "Z10", "U2", "Z11", "Z13", "P0", "Z12", "Z20", "Z21", "Z23", "L0", "Z22", "P1", "Z30", "Z31", "Z33",
    "R0", "Z32", "P2", "Z40", "L1", "G0", "Z41", "Z43", "Z42", "R1", "Z50", "P3", "Z51", "Z53", "L2", "G1", "Z52",
    "Z60", "R2", "Z61", "P4", "Z63", "G2", "Z62", "L3", "Z70", "E0", "Z71", "E1", "Z73", "L4", "R3", "Z72", "G3", "Z80",
    "R4", "E2", "G4", "P6", "Z81", "F0", "E3", "Z83", "F1", "Z82", "E4", "P7", "F2", "E5", "L6", "F3", "P8", "R6", "F4",
    "G6", "L7", "F5", "L8", "R7", "R5", "R8",
)


def kernel(
    og_ref, hid_hbm, w_hbm, ex_hbm, rw_hbm,
    hg_ref, wg_ref, rt_ref,
    hid_ref, w_ref, ex_ref, rw_ref,
    rows, raw, ht, hw, sel, wtok, sg, sgx, red,
    load, u_s, u_r, z_s, z_r, p_s, p_r, e_s, e_r, v_s, v_r, a_s, a_r, f_s, f_r, c_s, c_r, x_s, x_r, d_s, d_r,
):
    dp, ex = lax.axis_index("dp"), lax.axis_index("expert")
    z, ylo = dp // 2, dp % 2
    x, yhi, c = ex // 4, (ex // 2) % 2, ex % 2
    y = yhi * 2 + ylo
    u = y + c * (x - y)
    v = x + c * (y - x)

    def at(x, y, z, c):
        return {"dp": z * 2 + y % 2, "expert": (x * 2 + y // 2) * 2 + c}

    def along(du, dv, core=c):
        uu, vv = (u + du + 4) % 4, (v + dv + 4) % 4
        return at(vv + c * (uu - vv), uu + c * (vv - uu), z, core)

    def beside(dz):
        return at(x, y, (z + dz + Z) % Z, c)

    twin = at(x, y, z, 1 - c)

    barrier = pltpu.get_barrier_semaphore()
    greeted = [along(k, 0) for k in (1, 2, 3)] + [along(0, k) for k in (1, 3)]
    greeted += [beside(1), beside(-1), twin]
    for device in greeted:
        pl.semaphore_signal(barrier, inc=1, device_id=device, device_id_type=MESH)
    loads = [
        pltpu.make_async_copy(src, dst, load.at[i])
        for i, (src, dst) in enumerate(
            ((ex_hbm, ex_ref), (rw_hbm, rw_ref), (hid_hbm, hid_ref), (w_hbm, w_ref))
        )
    ]
    loads.append(pltpu.make_async_copy(og_ref, rows.at[0, c, v, u], load.at[4]))
    for op in loads:
        op.start()
    pl.semaphore_wait(barrier, len(greeted))
    loads[4].wait()

    sent = []

    def copy(src, dst, send, recv, device):
        return pltpu.make_async_remote_copy(
            src_ref=src, dst_ref=dst, send_sem=send, recv_sem=recv, device_id=device, device_id_type=MESH
        )

    def push(src, dst, send, recv, device):
        op = copy(src, dst, send, recv, device)
        op.start()
        sent.append(op)

    def arrived(dst, send, recv):
        copy(dst, dst, send, recv, twin).wait_recv()


    def piece(slot, vv, k):
        return rows.at[slot, c, vv, (u - k + 4) % 4]

    def z_send(d, k):
        for way in (0, 1):
            if d == 7 and way != k // 2:
                continue
            src = 0 if d == 0 else 2 * d - 1 + way
            dst = 15 if d == 7 else 2 * d + 1 + way
            push(piece(src, v, k), piece(dst, v, k), z_s.at[d, way, k], z_r.at[d, way, k], beside(1 - 2 * way))

    def z_wait(d, k):
        for way in (0, 1):
            if d == 8 and way != k // 2:
                continue
            dst = 15 if d == 8 else 2 * d - 1 + way
            arrived(piece(dst, v, k), z_s.at[d - 1, way, k], z_r.at[d - 1, way, k])

    def slot_list(d):
        return (0,) if d == 0 else (15,) if d == 8 else (2 * d - 1, 2 * d)

    def slots(d):
        return pl.ds(0, 1) if d == 0 else pl.ds(15, 1) if d == 8 else pl.ds(2 * d - 1, 2)

    def v_all(d, vv):
        return rows.at[slots(d), c, vv]

    def v_half(d, vv, way):
        if d in (0, 8):
            return rows.at[slots(d), c, vv, pl.ds(2 * way, 2)]
        return rows.at[pl.ds(2 * d - 1 + way, 1), c, vv]

    def v_send(d):
        for way in (0, 1):
            own = v_all(d, v)
            push(own, own, v_s.at[d, way], v_r.at[d, way], along(0, 1 - 2 * way))

    def v_piece(slot, k):
        at_slot = EARLY_SLOTS.index(slot)
        for way in (0, 1):
            push(piece(slot, v, k), piece(slot, v, k), p_s.at[at_slot, k, way], p_r.at[at_slot, k, way], along(0, 1 - 2 * way))

    def v_pass(d):
        for way in (0, 1):
            step = 1 - 2 * way
            vv = (v - step + 4) % 4
            if d in EARLY:
                for slot in slot_list(d):
                    for k in ORDER:
                        at_slot = EARLY_SLOTS.index(slot)
                        arrived(piece(slot, vv, k), p_s.at[at_slot, k, way], p_r.at[at_slot, k, way])
            else:
                arrived(v_all(d, vv), v_s.at[d, way], v_r.at[d, way])
            half = v_half(d, vv, way)
            push(half, half, a_s.at[d, way], a_r.at[d, way], along(0, step))
        if d == 8:
            for way in (0, 1):
                step = 1 - 2 * way
                half = v_half(d, (v - step + 4) % 4, way)
                push(half, half, f_s.at[way], f_r.at[way], along(0, step, 1 - c))

    def v_last(d):
        for way in (0, 1):
            arrived(v_half(d, (v + 2) % 4, way), a_s.at[d, way], a_r.at[d, way])

    def e_part(slot, unit):
        return rows.at[slot, c, (v + (1, 3, 2)[unit // 2]) % 4, pl.ds(2 * (unit % 2), 2)]

    def e_send(unit):
        for way in (0, 1):
            src, dst = e_part(2 * SKIP - 3 + way, unit), e_part(2 * SKIP - 1 + way, unit)
            push(src, dst, e_s.at[way, unit], e_r.at[way, unit], beside(1 - 2 * way))

    def e_wait(unit):
        for way in (0, 1):
            arrived(e_part(2 * SKIP - 1 + way, unit), e_s.at[way, unit], e_r.at[way, unit])

    def c_send(d, k):
        own = rows.at[slots(d), c, (v + k) % 4]
        push(own, own, c_s.at[d, k], c_r.at[d, k], twin)

    def c_wait(d):
        for k in (0, 1, 3) if d == 8 else (0, 1, 2, 3):
            arrived(rows.at[slots(d), 1 - c, (u + k) % 4], c_s.at[d, k], c_r.at[d, k])

    def prepare():
        mine = ex_ref[...] == ex
        hit = jnp.max(jnp.where(mine, 1.0, 0.0), axis=0, keepdims=True)
        wtok[...] = jnp.sum(jnp.where(mine, rw_ref[...], 0.0), axis=0, keepdims=True)
        hits = jnp.concatenate([hit[:, b * TOK : (b + 1) * TOK] for b in range(BLOCKS)], axis=0)
        upto = lax.broadcasted_iota(jnp.int32, (TOK, TOK), 0) <= lax.broadcasted_iota(jnp.int32, (TOK, TOK), 1)
        count = jnp.dot(hits.astype(BF16), jnp.where(upto, 1.0, 0.0).astype(BF16), preferred_element_type=F32)
        code = jnp.where(hits > 0, count - 1.0, -1000.0)
        slot = lax.broadcasted_iota(jnp.int32, (2 * MOST, 2 * TOK), 0).astype(F32)
        for j in range(BLOCKS // 2):
            both = jnp.concatenate([code[2 * j : 2 * j + 1], code[2 * j + 1 : 2 * j + 2] + float(MOST)], axis=1)
            one = jnp.where(slot == both, 1.0, 0.0).astype(BF16)
            sel[j] = one
            tokens = pl.ds(j * 2 * TOK, 2 * TOK)
            part = jnp.dot(hid_ref[0, :, pl.ds(j * TOK, TOK)], one, preferred_element_type=F32)
            ht[:, tokens] = part.astype(BF16)
            hw[:, tokens] = (part * wtok[:, tokens]).astype(BF16)

    def places(d):
        if d == 0:
            return ((0, z),)
        if d == 8:
            return ((15, (z + 8) % Z),)
        return ((2 * d - 1, (z - d + Z) % Z), (2 * d, (z + d) % Z))

    def columns(zi):
        return pl.ds(pl.multiple_of(zi * FEAT, 128), FEAT)

    def block(s, xx, yh, core):
        if core == 0:
            return rows[s, 0, xx, 2 * yh : 2 * yh + 2].reshape(FEAT, TOK)
        return jnp.concatenate([rows[s, 1, 2 * yh, xx], rows[s, 1, 2 * yh + 1, xx]], axis=0)

    def slab(s, xx):
        return jnp.concatenate([block(s, xx, b // 2, b % 2) for b in range(4)], axis=1)

    def add_raw(d, first):
        here = places(d)
        w = jnp.concatenate([w_ref[0, :, columns(zi)] for _, zi in here], axis=1)

        for xx in range(4):
            t = jnp.concatenate([slab(s, xx) for s, _ in here], axis=0)
            tokens = pl.ds(xx * 4 * TOK, 4 * TOK)
            more = jnp.dot(w, t, preferred_element_type=F32)
            raw[:, tokens] = more if first else raw[:, tokens] + more

    def add_last(core):
        w = w_ref[0, :, columns((z + 8) % Z)]

        for xx in range(4):
            t = jnp.concatenate([block(15, xx, yh, core) for yh in (0, 1)], axis=1)
            more = jnp.dot(w, t, preferred_element_type=F32)
            for yh in (0, 1):
                tokens = pl.ds((4 * xx + 2 * yh + core) * TOK, TOK)
                raw[:, tokens] += more[:, yh * TOK : (yh + 1) * TOK]

    def put_grad(d):
        here = places(d)
        t = jnp.concatenate(
            [jnp.concatenate([slab(s, xx) for xx in range(4)], axis=1) for s, _ in here], axis=0
        )
        grad = lax.dot_general(hw[...], t, NT, preferred_element_type=F32).astype(BF16)
        for i, (_, zi) in enumerate(here):
            wg_ref[0, :, columns(zi)] = grad[:, i * FEAT : (i + 1) * FEAT]

    for k in (1, 3, 2):
        push(piece(0, v, 0), piece(0, v, 0), u_s.at[k - 1], u_r.at[k - 1], along(k, 0))
    z_send(0, 0)
    v_piece(0, 0)
    for op in loads[:3]:
        op.wait()
    prepare()
    loads[3].wait()

    def on_u(k):
        arrived(piece(0, v, k), u_s.at[k - 1], u_r.at[k - 1])
        z_send(0, k)
        v_piece(0, k)
        if k == ORDER[3]:
            c_send(0, 0)

    def on_z(d, k):
        z_wait(d, k)
        if d < 8:
            z_send(d, k)
        if d in EARLY:
            for slot in slot_list(d):
                v_piece(slot, k)
        if k == ORDER[3]:
            if d not in EARLY and d != SKIP:
                v_send(d)
            c_send(d, 0)

    def on_v(d):
        v_pass(d)
        c_send(d, 1)
        c_send(d, 3)

    def on_far(d):
        v_last(d)
        if d < 8:
            c_send(d, 2)

    def on_e(unit):
        e_wait(unit)
        if unit % 2 == 1:
            c_send(SKIP, (1, 3, 2)[unit // 2])

    summed = []
    for step in PLAN:
        kind, d = step[0], int(step[1])
        if kind == "U":
            on_u(d)
        elif kind == "Z":
            on_z(d, int(step[2]))
        elif kind == "P":
            on_v(d)
        elif kind == "L":
            on_far(d)
        elif kind == "E":
            e_send(d)
        elif kind == "F":
            on_e(d)
        elif kind == "R" and d == 8:
            continue
        elif kind == "R":
            c_wait(d)
            add_raw(d, not summed)
            summed.append(d)
        else:
            put_grad(d)

    def tell(core, first):
        for i in range(BLOCKS // 2):
            b = 2 * i + core
            tokens = pl.ds(pl.multiple_of(b * TOK, TOK), TOK)
            share = jnp.sum(ht[:, tokens].astype(F32) * raw[:, tokens], axis=0, keepdims=True)
            sg[b] = jnp.broadcast_to(share, (8, TOK))
        for k in range(first, BLOCKS, 2):
            to = (ex + k) % BLOCKS
            push(sg.at[to], sgx.at[ex], x_s.at[k], x_r.at[k], {"dp": dp, "expert": to})

    for core in (0, 1):
        pl.when(c == core)(functools.partial(add_last, core))
    tell(c, 2)
    c_wait(8)
    for way in (0, 1):
        arrived(rows.at[slots(8), 1 - c, (u + 2) % 4, pl.ds(2 * way, 2)], f_s.at[way], f_r.at[way])
    for core in (0, 1):
        pl.when(c != core)(functools.partial(add_last, core))
    tell(1 - c, 1)
    sgx[ex] = sg[ex]
    for d in LATE[::2]:
        put_grad(d)
    named = ex_ref[:, pl.ds(pl.multiple_of(ex * TOK, TOK), TOK)]
    total = jnp.zeros((4, TOK), F32)
    for k in range(1, BLOCKS):
        arrived(sgx.at[(ex - k + BLOCKS) % BLOCKS], x_s.at[k], x_r.at[k])
    for e in range(BLOCKS):
        total = total + jnp.where(named == e, sgx[e, 0:1, :], 0.0)
    red[dp] = total
    before = len(sent)
    for k in sorted(range(1, 2 * Z), key=lambda k: -min(k, 2 * Z - k)):
        push(red.at[dp], red.at[dp], d_s.at[k], d_r.at[k], {"dp": (dp + k) % (2 * Z), "expert": ex})
    for d in LATE[1::2]:
        put_grad(d)
    for j in range(BLOCKS // 2):
        tokens = pl.ds(j * 2 * TOK, 2 * TOK)
        grad = (raw[:, tokens] * wtok[:, tokens]).astype(BF16)
        hg_ref[0, :, pl.ds(j * TOK, TOK)] = lax.dot_general(grad, sel[j], NT, preferred_element_type=F32).astype(BF16)
    for op in sent[:before]:
        op.wait_send()
    for k in range(1, 2 * Z):
        arrived(red.at[(dp - k + 2 * Z) % (2 * Z)], d_s.at[k], d_r.at[k])
    total = red[0]
    for k in range(1, 2 * Z):
        total = total + red[k]
    rt_ref[...] = total
    for op in sent[before:]:
        op.wait_send()


def hand_over(hg_ref, wg_ref, rt_ref, hg_out, wg_out, rt_out, sems):
    width = wg_ref.shape[2] // 4
    copies = [(wg_ref.at[:, :, pl.ds(i * width, width)], wg_out.at[:, :, pl.ds(i * width, width)]) for i in range(4)]
    copies += [(hg_ref, hg_out), (rt_ref, rt_out)]
    copies = [pltpu.make_async_copy(src, dst, sems.at[i]) for i, (src, dst) in enumerate(copies)]
    for op in copies:
        op.start()
    for op in copies:
        op.wait()


def body(out_grad, hidden, down_weight, experts, route_weight):
    vmem = pl.BlockSpec(memory_space=pltpu.VMEM)
    dma = pltpu.SemaphoreType.DMA
    operands = (out_grad.T, hidden.swapaxes(1, 2), down_weight, experts.T, route_weight.T)
    shapes = (
        jax.ShapeDtypeStruct((1, FFD, BLOCKS * MOST), BF16),
        jax.ShapeDtypeStruct(down_weight.shape, BF16),
        jax.ShapeDtypeStruct((4, TOK), F32),
    )
    results = pl.pallas_call(
        kernel,
        out_shape=shapes,
        in_specs=[pl.BlockSpec(memory_space=pltpu.HBM)] * 5,
        out_specs=(vmem,) * 3,
        scratch_shapes=[
            pltpu.VMEM((1, FFD, BLOCKS * MOST), BF16),
            pltpu.VMEM(down_weight.shape, BF16),
            pltpu.VMEM((4, TOKENS), jnp.int32),
            pltpu.VMEM((4, TOKENS), F32),
            pltpu.VMEM((Z, 2, 4, 4, PIECE, TOK), BF16),
            pltpu.VMEM((FFD, TOKENS), F32),
            pltpu.VMEM((FFD, TOKENS), BF16),
            pltpu.VMEM((FFD, TOKENS), BF16),
            pltpu.VMEM((BLOCKS // 2, 2 * MOST, 2 * TOK), BF16),
            pltpu.VMEM((1, TOKENS), F32),
            pltpu.VMEM((BLOCKS, 8, TOK), F32),
            pltpu.VMEM((BLOCKS, 8, TOK), F32),
            pltpu.VMEM((2 * Z, 4, TOK), F32),
            dma((5,)),
            dma((3,)), dma((3,)),
            dma((8, 2, 4)), dma((8, 2, 4)),
            dma((7, 4, 2)), dma((7, 4, 2)),
            dma((2, 6)), dma((2, 6)),
            dma((GROUPS, 2)), dma((GROUPS, 2)),
            dma((GROUPS, 2)), dma((GROUPS, 2)),
            dma((2,)), dma((2,)),
            dma((GROUPS, 4)), dma((GROUPS, 4)),
            dma((BLOCKS,)), dma((BLOCKS,)),
            dma((2 * Z,)), dma((2 * Z,)),
        ],
        compiler_params=pltpu.CompilerParams(
            collective_id=0, has_side_effects=True, vmem_limit_bytes=42 << 20
        ),
        cost_estimate=pl.CostEstimate(flops=8 * 10**9, bytes_accessed=30 * 10**6, transcendentals=0),
        name="broadcast_grads",
    )(*(pltpu.with_memory_space_constraint(a, pltpu.HBM) for a in operands))
    hidden_grad, weight_grad, route = pl.pallas_call(
        hand_over,
        out_shape=shapes,
        in_specs=[pl.BlockSpec(memory_space=pl.ANY)] * 3,
        out_specs=(pl.BlockSpec(memory_space=pltpu.HBM),) * 3,
        scratch_shapes=[dma((6,))],
        compiler_params=pltpu.CompilerParams(vmem_limit_bytes=1 << 20),
        name="hand_over",
    )(*results)
    return hidden_grad.swapaxes(1, 2), weight_grad, route.T


def solution(mesh):
    placed = (P("expert", "dp"), P("expert", None, "dp"), P("expert", "dp", None), P(), P())
    return jax.shard_map(
        body,
        mesh=mesh,
        in_specs=placed,
        out_specs=(P("expert", None, "dp"), P("expert", "dp", None), P("expert", None)),
        check_vma=False,
    )
```
